32 devices in a mesh: grp: 4 (over z), head: 8 (over y, x, core).
Axes of the slice: x: 2, y: 2, z: 4, core: 2. Of those that a mesh axis runs over, the one named last changes fastest.
Arguments:
- queries: bfloat16 [8, 8, 4096], P('head'), may hold values from -1500 to 1500
- shared_prefix_keys: bfloat16 [8, 512, 512], P('head', 'grp'), may hold values from -6 to 6
- shared_prefix_values: bfloat16 [8, 512, 512], P('head', 'grp'), may hold values from -6 to 6
- row_suffix_keys: bfloat16 [8, 8, 16, 512], P('head', 'grp'), may hold values from -6 to 6
- row_suffix_values: bfloat16 [8, 8, 16, 512], P('head', 'grp'), may hold values from -6 to 6
- suffix_lengths: int32 [8, 8], P('head', 'grp'), may hold values from 1 to 16, as said below
- residual: bfloat16 [8, 8, 2048], P('head', 'grp'), may hold values from -4 to 4
- out_weight: bfloat16 [4096, 2048], P('head'), may hold values from -0.5 to 0.5
- norm_gain: float32 [2048], replicated, may hold values from 0.5 to 2
- router_weight: bfloat16 [2048, 16], replicated, may hold values from -0.125 to 0.125
- gate_weights: bfloat16 [16, 2048, 384], P('head'), may hold values from -0.125 to 0.125
- up_weights: bfloat16 [16, 2048, 384], P('head'), may hold values from -0.125 to 0.125
- down_weights: bfloat16 [16, 384, 2048], P('head'), may hold values from -0.3125 to 0.3125
- expert_ids: int32 [8, 8, 8], P('head', 'grp'), may hold values from 0 to 15, all different within a row; in each aligned block of 2 rows (0 to 1, 2 to 3, ..., all dimensions but the last counted through in order) at most 2 rows name the same one
Outputs:
- layer_out: float32 [8, 8, 2048], P('head', 'grp')
The draws below stay inside these ranges and needn't reach their ends.
Inputs may be any that keep to these rules, and one draw needn't show every extreme that they name: `expert_ids`: each row names 8 different experts; in each aligned block of 2 rows (the rows of one device, prompts then rows in order) no expert is named by more than 2 rows, a bound that some block reaches. `suffix_lengths`: every prompt has a row whose suffix holds 16 tokens.
All inputs are finite; a program needn't handle non-finite values.
Results may differ from the reference program's by a relative error of at most 0.007.
Values may be sent and summed in bfloat16 or wider, within the bound.
A program may use at most 128 MiB of HBM per device.

```python
import math
import jax
import jax.numpy as jnp
import numpy as np
from jax import lax

D = 2048
QUERY_HEADS = 32
KEY_VALUE_HEADS = 4
HEAD_SIZE = 128
FF = 384
EXPERTS = 16
TOPK = 8
SUFFIX_MAXIMUM = 16
ROW_DEV = 2
CAP = 2
PREFIX_LENGTH = 512
PROMPT_ROWS = 8
PROMPT_COUNT = 8


def draw_pair(key):
    key_portion = jax.random.fold_in(key, 101)
    query_part = jax.random.fold_in(key, 202)
    scale_part = jax.random.fold_in(key, 404)
    rows_of_keys = jnp.clip(jax.random.normal(key_portion, (PROMPT_COUNT, PREFIX_LENGTH, KEY_VALUE_HEADS * HEAD_SIZE), jnp.float32), -6.0, 6.0)
    base_queries = jnp.clip(jax.random.normal(query_part, (PROMPT_COUNT, PROMPT_ROWS, QUERY_HEADS, HEAD_SIZE), jnp.float32), -6.0, 6.0)
    head_scale = jnp.exp(jax.random.uniform(scale_part, (PROMPT_COUNT, PROMPT_ROWS, QUERY_HEADS, 1), jnp.float32, math.log(0.5), math.log(16.0)))
    query_rows = (base_queries * head_scale).reshape(PROMPT_COUNT, PROMPT_ROWS, QUERY_HEADS * HEAD_SIZE)
    return (rows_of_keys, query_rows)


def draw_queries(key, part):
    return draw_pair(key)[1].astype(jnp.bfloat16)


def draw_shared_prefix_keys(key, part):
    return draw_pair(key)[0].astype(jnp.bfloat16)


def draw_suffix_lengths(key, part):
    base_lengths = jax.random.randint(jax.random.fold_in(key, 7), (PROMPT_COUNT, PROMPT_ROWS), 1, SUFFIX_MAXIMUM + 1)
    long_row = jax.random.randint(jax.random.fold_in(key, 8), (PROMPT_COUNT,), 0, PROMPT_ROWS)
    is_long = jnp.arange(PROMPT_ROWS)[None, :] == long_row[:, None]
    return jnp.where(is_long, SUFFIX_MAXIMUM, base_lengths).astype(jnp.int32)


def level_of(key, dims, pieces, low, largest):
    level, own = 1.0, jax.random.fold_in(key, 6)
    for position, blocks in pieces:
        draws = jnp.exp(jax.random.uniform(jax.random.fold_in(own, position), (blocks,), jnp.float32, low / len(pieces), largest / len(pieces)))
        level = level * jnp.repeat(draws, dims[position] // blocks).reshape([-1 if axis == position else 1 for axis in range(len(dims))])
    return level


def deal_out(key, own, number, rows, number_of, top, reach, slope):
    sequence = jax.random.permutation(key, number_of)
    heavy_load, common = load_shares(number_of, rows * top, reach, slope, True), load_shares(number_of, rows * top, reach, slope, False)
    places = jnp.arange(number_of)

    def named(lengths, turn):
        used = int((lengths > 0).sum())
        fixed = max(1, used // 4)
        passed = fixed + (places - fixed + turn * (used - fixed)) % max(1, number_of - fixed)
        return jnp.zeros((number_of,), jnp.int32).at[sequence[jnp.where(places < fixed, places, passed)]].set(jnp.asarray(lengths, jnp.int32))

    lengths = jnp.where(number % 4 == 0, named(heavy_load, number // 4), named(common, number - number // 4 - 1))
    mixed = jax.random.permutation(jax.random.fold_in(own, 3), number_of)
    source_of, sink = mixed[0:number_of // 2 * 2:2], mixed[1:number_of // 2 * 2:2]
    room = jnp.minimum(lengths[source_of] - 1, reach - lengths[sink]) // 2
    room = jnp.where((source_of == sequence[0]) | (sink == sequence[0]) | (lengths[sink] == 0), 0, jnp.maximum(room, 0))
    passed = jax.random.randint(jax.random.fold_in(own, 4), (number_of // 2,), 0, 1 << 20) % (room + 1)
    lengths = lengths.at[source_of].add(-passed).at[sink].add(passed)
    labels = jnp.searchsorted(jnp.cumsum(lengths), jnp.arange(rows * top), side="right").astype(jnp.int32)
    listing = labels.reshape(top, rows).T
    listing = listing[jax.random.permutation(jax.random.fold_in(own, 1), rows)]
    turn = jax.random.randint(jax.random.fold_in(own, 2), (rows, 1), 0, top)
    return jnp.take_along_axis(listing, (jnp.arange(top)[None, :] + turn) % top, axis=1)


def load_shares(number_of, total, limit, lean, full):
    portions = [(1 << 20) // math.isqrt(rank ** lean) + 1 for rank in range(1, number_of + 1)]
    largest = limit if full else min(limit, max(-(-total // number_of), total * portions[0] // sum(portions)))
    least = 1 if total - largest >= number_of - 1 else 0
    holding, spare = [largest] + [least] * (number_of - 1), total - largest - least * (number_of - 1)
    while spare > 0:
        movable = [i for i in range(1, number_of) if holding[i] < largest] or [i for i in range(1, number_of) if holding[i] < limit]
        mass, remaining = sum([portions[i] for i in movable]), spare
        for i in movable:
            more = min(limit - holding[i], max(1, remaining * portions[i] // mass), spare)
            holding[i] = holding[i] + more
            spare = spare - more
    return np.array(holding)


def bell_draw(rng, shape, scale, reach, pieces=(), held_as=jnp.bfloat16):
    entries = jax.random.normal(rng, shape, jnp.float32) * scale
    if len(pieces) > 0:
        entries = level_of(rng, shape, pieces, -0.22, 0.18) * entries
    return jnp.clip(entries, min=-reach, max=reach).astype(held_as)


def setup_inputs(seed: int = 0) -> dict:
    arg_keys = jax.random.split(jax.random.key(seed), 15)
    queries = draw_queries(jax.random.fold_in(arg_keys[14], 71), 0)
    shared_prefix_keys = draw_shared_prefix_keys(jax.random.fold_in(arg_keys[14], 71), 0)
    shared_prefix_values = bell_draw(arg_keys[2], (PROMPT_COUNT, PREFIX_LENGTH, KEY_VALUE_HEADS * HEAD_SIZE), 1.0, 6.0, ((0, 8), (1, 4)))
    row_suffix_keys = bell_draw(arg_keys[3], (PROMPT_COUNT, PROMPT_ROWS, SUFFIX_MAXIMUM, KEY_VALUE_HEADS * HEAD_SIZE), 1.0, 6.0, ((0, 8), (1, 4)))
    row_suffix_values = bell_draw(arg_keys[4], (PROMPT_COUNT, PROMPT_ROWS, SUFFIX_MAXIMUM, KEY_VALUE_HEADS * HEAD_SIZE), 1.0, 6.0, ((0, 8), (1, 4)))
    suffix_lengths = draw_suffix_lengths(jax.random.fold_in(arg_keys[14], 71), 0)
    residual = bell_draw(arg_keys[6], (PROMPT_COUNT, PROMPT_ROWS, D), 0.5, 4.0, ((0, 8), (1, 4)))
    out_weight = bell_draw(arg_keys[7], (QUERY_HEADS * HEAD_SIZE, D), HEAD_SIZE ** -0.5, 0.5, ((0, 8),))
    norm_gain = jnp.clip(jnp.exp(jax.random.uniform(arg_keys[8], (D,), jnp.float32, math.log(0.5), math.log(2.0))), 0.5, 2.0)
    router_weight = bell_draw(arg_keys[9], (D, EXPERTS), D ** -0.5, 0.125)
    gate_weights = bell_draw(arg_keys[10], (EXPERTS, D, FF), D ** -0.5, 0.125, ((0, 8),))
    up_weights = bell_draw(arg_keys[11], (EXPERTS, D, FF), D ** -0.5, 0.125, ((0, 8),))
    down_weights = bell_draw(arg_keys[12], (EXPERTS, FF, D), FF ** -0.5, 0.3125, ((0, 8),))
    expert_ids_keys = jax.random.split(jax.random.fold_in(arg_keys[13], 1), PROMPT_COUNT * PROMPT_ROWS // ROW_DEV)
    expert_ids_turns = jax.random.permutation(jax.random.fold_in(arg_keys[13], 3), PROMPT_COUNT * PROMPT_ROWS // ROW_DEV)
    expert_ids = jax.vmap(lambda own, number: deal_out(jax.random.fold_in(arg_keys[13], 2), own, number, ROW_DEV, EXPERTS, TOPK, CAP, 2))(expert_ids_keys, expert_ids_turns).reshape((PROMPT_COUNT, PROMPT_ROWS, TOPK))
    return {"queries": queries, "shared_prefix_keys": shared_prefix_keys, "shared_prefix_values": shared_prefix_values, "row_suffix_keys": row_suffix_keys, "row_suffix_values": row_suffix_values, "suffix_lengths": suffix_lengths, "residual": residual, "out_weight": out_weight, "norm_gain": norm_gain, "router_weight": router_weight, "gate_weights": gate_weights, "up_weights": up_weights, "down_weights": down_weights, "expert_ids": expert_ids}


masked_score = -1e+30
norm_epsilon = 1e-06

def reference(queries, shared_prefix_keys, shared_prefix_values, row_suffix_keys, row_suffix_values, suffix_lengths, residual, out_weight, norm_gain, router_weight, gate_weights, up_weights, down_weights, expert_ids):
    query_group_width = QUERY_HEADS // KEY_VALUE_HEADS
    score_scale = 1.0 / math.sqrt(HEAD_SIZE)

    def one_prompt(prompt_parts):
        query_tile, key_tile, value_tile, suffix_key_rows, suffix_value_rows, row_lengths = prompt_parts
        heads_of_queries = query_tile.astype(jnp.float32).reshape(PROMPT_ROWS, KEY_VALUE_HEADS, query_group_width, HEAD_SIZE)
        heads_of_keys = key_tile.astype(jnp.float32).reshape(PREFIX_LENGTH, KEY_VALUE_HEADS, HEAD_SIZE)
        heads_of_values = value_tile.astype(jnp.float32).reshape(PREFIX_LENGTH, KEY_VALUE_HEADS, HEAD_SIZE)
        suffix_key_heads = suffix_key_rows.astype(jnp.float32).reshape(PROMPT_ROWS, SUFFIX_MAXIMUM, KEY_VALUE_HEADS, HEAD_SIZE)
        suffix_value_heads = suffix_value_rows.astype(jnp.float32).reshape(PROMPT_ROWS, SUFFIX_MAXIMUM, KEY_VALUE_HEADS, HEAD_SIZE)
        pre_scores = jnp.einsum('rkgd,pkd->rkgp', heads_of_queries, heads_of_keys) * score_scale
        in_suffix = (jnp.arange(SUFFIX_MAXIMUM)[None, :] < row_lengths[:, None])[:, None, None, :]
        suf_scores = jnp.einsum('rkgd,rskd->rkgs', heads_of_queries, suffix_key_heads) * score_scale
        suf_scores = jnp.where(in_suffix, suf_scores, masked_score)
        top_score = jnp.maximum(lax.optimization_barrier(jnp.max(pre_scores, -1)), lax.optimization_barrier(jnp.max(suf_scores, -1)))
        pre_terms = jnp.exp(pre_scores - top_score[..., None])
        suf_terms = jnp.where(in_suffix, jnp.exp(suf_scores - top_score[..., None]), 0.0)
        total_mass = lax.optimization_barrier(jnp.sum(pre_terms, -1)) + lax.optimization_barrier(jnp.sum(suf_terms, -1))
        pre_round = lax.optimization_barrier(pre_terms.astype(jnp.bfloat16)).astype(jnp.float32)
        suf_round = lax.optimization_barrier(suf_terms.astype(jnp.bfloat16)).astype(jnp.float32)
        weighted = jnp.einsum('rkgp,pkd->rkgd', pre_round, heads_of_values) + jnp.einsum('rkgs,rskd->rkgd', suf_round, suffix_value_heads)
        return (weighted / total_mass[..., None]).reshape(PROMPT_ROWS, QUERY_HEADS * HEAD_SIZE).astype(jnp.bfloat16)
    attention = lax.map(one_prompt, (queries, shared_prefix_keys, shared_prefix_values, row_suffix_keys, row_suffix_values, suffix_lengths))
    row_total = PROMPT_COUNT * PROMPT_ROWS
    flat_attn = attention.reshape(row_total, QUERY_HEADS * HEAD_SIZE)
    projected = jnp.dot(flat_attn, out_weight, preferred_element_type=jnp.float32)
    hidden_state = residual.reshape(row_total, D).astype(jnp.float32) + projected
    mean_square = lax.optimization_barrier(jnp.mean(hidden_state * hidden_state, -1, keepdims=True))
    normed = (hidden_state * lax.rsqrt(mean_square + norm_epsilon) * norm_gain).astype(jnp.bfloat16)
    logits = jnp.dot(normed, router_weight, preferred_element_type=jnp.float32)
    chosen_ids = expert_ids.reshape(row_total, TOPK)
    chosen_logits = jnp.take_along_axis(logits, chosen_ids, 1)
    expo_terms = jnp.exp(chosen_logits)
    route_weights = expo_terms / lax.optimization_barrier(jnp.sum(expo_terms, -1, keepdims=True))
    block_count = row_total // ROW_DEV
    per_block = ROW_DEV * TOPK
    assigned = chosen_ids.reshape(block_count, per_block)
    one_hot = (assigned[..., None] == jnp.arange(EXPERTS, dtype=jnp.int32)).astype(jnp.int32)
    earlier = jnp.cumsum(one_hot, 1) - one_hot
    slot_index = lax.optimization_barrier(jnp.sum(earlier * one_hot, -1)).astype(jnp.int32)
    row_index = (jnp.arange(block_count, dtype=jnp.int32)[:, None] * ROW_DEV + jnp.arange(per_block, dtype=jnp.int32)[None, :] // TOPK).astype(jnp.int32)
    block_index = jnp.broadcast_to(jnp.arange(block_count, dtype=jnp.int32)[:, None], (block_count, per_block))
    row_table = jnp.full((EXPERTS, block_count, CAP), row_total, jnp.int32).at[assigned, block_index, slot_index].set(row_index)
    weight_table = jnp.zeros((EXPERTS, block_count, CAP), jnp.float32).at[assigned, block_index, slot_index].set(route_weights.reshape(block_count, per_block))
    padded = jnp.concatenate([normed, jnp.zeros((1, D), jnp.bfloat16)], 0)

    def expert_step(accumulated, expert_parts):
        row_slots, slot_weights, gate_matrix, up_matrix, down_matrix = expert_parts
        flat_slots = row_slots.reshape(-1)
        picked = padded[flat_slots]
        gate_out = jnp.dot(picked, gate_matrix, preferred_element_type=jnp.float32)
        up_out = jnp.dot(picked, up_matrix, preferred_element_type=jnp.float32)
        hidden_act = (jax.nn.silu(gate_out) * up_out).astype(jnp.bfloat16)
        expert_out = jnp.dot(hidden_act, down_matrix, preferred_element_type=jnp.float32).astype(jnp.bfloat16)
        expert_out = lax.optimization_barrier(expert_out).astype(jnp.float32)
        accumulated = accumulated.at[flat_slots].add(slot_weights.reshape(-1)[:, None] * expert_out)
        return (accumulated, None)
    accumulated, _ = lax.scan(expert_step, jnp.zeros((row_total + 1, D), jnp.float32), (row_table, weight_table, gate_weights, up_weights, down_weights))
    layer_out = hidden_state + accumulated[:row_total]
    return layer_out.reshape(PROMPT_COUNT, PROMPT_ROWS, D)
```

```python
import functools
import math

import jax
import jax.numpy as jnp
from jax import lax
from jax.experimental import pallas as pl
from jax.experimental.pallas import tpu as pltpu
from jax.sharding import PartitionSpec as P

QUERY_HEADS = 32
KEY_VALUE_HEADS = 4
HEAD_SIZE = 128
TOPK = 8

masked_score = -1e30
norm_epsilon = 1e-06
f32, bf16, i32 = jnp.float32, jnp.bfloat16, jnp.int32
MESH = pl.DeviceIdType.MESH


def dot(a, b):
    return jnp.dot(a, b, preferred_element_type=f32)


def dot_nt(a, b):
    return lax.dot_general(a, b, (((1,), (1,)), ((), ())), preferred_element_type=f32)


def one_hot(shape, source):
    a = lax.broadcasted_iota(i32, shape, 0)
    b = lax.broadcasted_iota(i32, shape, 1)
    col = lax.broadcasted_iota(i32, shape, 2)
    hit = jnp.where(source(a, b) == col, 1.0, 0.0).astype(f32)
    return hit.reshape(shape[0] * shape[1], shape[2]).astype(bf16)


def kernel(
    G,
    H,
    q_hbm,
    k_hbm,
    v_hbm,
    sk_hbm,
    sv_hbm,
    len_hbm,
    res_hbm,
    ow_hbm,
    gain_hbm,
    rw_hbm,
    gw_hbm,
    uw_hbm,
    dw_hbm,
    ids_hbm,
    out_ref,
    q_ref,
    k_ref,
    v_ref,
    sk_ref,
    sv_ref,
    len_ref,
    res_ref,
    ow_ref,
    gain_ref,
    rw_ref,
    gw_ref,
    uw_ref,
    dw_ref,
    ids_ref,
    s1,
    r1,
    s2,
    r2,
    s3,
    r3,
    s4,
    r4,
    gain_cr,
    res_cr,
    load_sem,
    send_sem,
    recv_sem,
):
    N = G * H
    g = lax.axis_index("grp")
    h = lax.axis_index("head")
    me = h * G + g

    rows = q_ref.shape[1]
    own = res_ref.shape[1]
    width = res_ref.shape[2]
    suffix = sk_ref.shape[2]
    group = QUERY_HEADS // KEY_VALUE_HEADS
    heads_dev = QUERY_HEADS // H
    per_group = group // heads_dev
    slot_rows = s1.shape[1] // 2
    chunks, chunk_width = 16 // own, s2.shape[2]
    all_rows = H * own
    local_experts = gw_ref.shape[0]
    experts = rw_ref.shape[1]

    pairs = [
        (q_hbm, q_ref),
        (k_hbm, k_ref),
        (len_hbm, len_ref),
        (sk_hbm, sk_ref),
        (v_hbm, v_ref),
        (sv_hbm, sv_ref),
        (res_hbm, res_ref),
        (gain_hbm, gain_ref),
        (ids_hbm, ids_ref),
        (ow_hbm, ow_ref),
        (rw_hbm, rw_ref),
        (gw_hbm, gw_ref),
        (uw_hbm, uw_ref),
        (dw_hbm, dw_ref),
    ]
    loads = [pltpu.make_async_copy(a, b, load_sem.at[i]) for i, (a, b) in enumerate(pairs)]
    for load in loads:
        load.start()

    barrier = pltpu.get_barrier_semaphore()

    def greet(i, carry):
        d = lax.rem(me + i, N)
        pl.semaphore_signal(
            barrier, inc=1, device_id=(lax.rem(d, G), lax.div(d, G)), device_id_type=MESH
        )
        return carry

    lax.fori_loop(1, N, greet, 0)

    def query_source(a, b):
        if per_group == 1:
            head_block, block = 0, a
        else:
            head_block, block = lax.div(a, G), lax.rem(a, G)
        head, row = lax.div(b, own), lax.rem(b, own)
        found = (head_block * heads_dev + head) * rows + block * own + row
        return jnp.where(b < heads_dev * own, found, -1)

    to_slots = one_hot((per_group * G, slot_rows, group * rows), query_source)
    to_heads = one_hot(
        (heads_dev, all_rows, H * slot_rows),
        lambda a, b: lax.div(b, own) * slot_rows + a * own + lax.rem(b, own),
    )
    to_owner = one_hot(
        (H, 16, chunks * all_rows),
        lambda a, b: lax.div(b, own) * all_rows + a * own + lax.rem(b, own),
    )
    to_chunks = one_hot(
        (chunks, all_rows, H * 16),
        lambda a, b: lax.div(b, own) * 16 + a * own + lax.rem(b, own),
    )
    stat_row = lax.broadcasted_iota(i32, (HEAD_SIZE, 2 * HEAD_SIZE), 0)
    stat_col = lax.broadcasted_iota(i32, (HEAD_SIZE, 2 * HEAD_SIZE), 1)
    spread = (
        jnp.where(
            jnp.where(stat_row < 3, 0, jnp.where(stat_row < 6, 1, 2))
            == jnp.where(stat_col < HEAD_SIZE, 0, 1),
            1.0,
            0.0,
        )
        .astype(f32)
        .astype(bf16)
    )

    for load in loads[:6]:
        load.wait()
    scale = 1.0 / math.sqrt(HEAD_SIZE)
    count = per_group * G * slot_rows
    mask_shape = (per_group * G, slot_rows, own * suffix)
    block = lax.broadcasted_iota(i32, mask_shape, 0)
    if per_group > 1:
        block = lax.rem(block, G)
    row = lax.rem(lax.broadcasted_iota(i32, mask_shape, 1), own)
    column = lax.broadcasted_iota(i32, mask_shape, 2)
    bound = jnp.zeros(mask_shape, i32)
    for r in range(own):
        bound = jnp.where(row == r, r * suffix + len_ref[0, r], bound)
    bound = jnp.where(block == g, bound, 0).reshape(count, own * suffix)
    first = (row * suffix).reshape(count, own * suffix)
    column = column.reshape(count, own * suffix)
    in_suffix = (column >= first) & (column < bound)
    lane = lax.broadcasted_iota(i32, (count, HEAD_SIZE), 1)
    q32 = q_ref[0].astype(f32)
    for k in range(KEY_VALUE_HEADS):
        cut = slice(k * HEAD_SIZE, (k + 1) * HEAD_SIZE)
        stacked = jnp.concatenate(
            [
                q32[:, j * HEAD_SIZE : (j + 1) * HEAD_SIZE]
                for j in range(k * group, (k + 1) * group)
            ],
            0,
        ).astype(bf16)
        query = dot(to_slots, stacked).astype(bf16)
        scores = dot_nt(query, k_ref[0, :, cut]) * scale
        suf = dot_nt(query, sk_ref[0, :, :, cut].reshape(own * suffix, HEAD_SIZE)) * scale
        suf = jnp.where(in_suffix, suf, masked_score)
        peak = jnp.maximum(
            jnp.max(scores, -1, keepdims=True), jnp.max(suf, -1, keepdims=True)
        )
        terms = jnp.exp(scores - peak)
        suf_terms = jnp.where(in_suffix, jnp.exp(suf - peak), 0.0)
        mass = jnp.sum(terms, -1, keepdims=True) + jnp.sum(suf_terms, -1, keepdims=True)
        weighted = dot(terms.astype(bf16), v_ref[0, :, cut]) + dot(
            suf_terms.astype(bf16), sv_ref[0, :, :, cut].reshape(own * suffix, HEAD_SIZE)
        )
        value = jnp.where(lane < 3, peak, mass)
        top = value.astype(bf16).astype(f32)
        rest = value - top
        middle = rest.astype(bf16).astype(f32)
        low = rest - middle
        piece = jnp.where(
            (lane == 0) | (lane == 3), top, jnp.where((lane == 1) | (lane == 4), middle, low)
        )
        piece = jnp.where(lane < 6, piece, 0.0)
        message = jnp.concatenate(
            [
                weighted.reshape(per_group * G, slot_rows, HEAD_SIZE),
                piece.reshape(per_group * G, slot_rows, HEAD_SIZE),
            ],
            1,
        )
        s1[k * per_group * G : (k + 1) * per_group * G] = message.astype(bf16)

    pl.semaphore_wait(barrier, N - 1)

    def send_state(i, carry):
        d = lax.rem(me + i, N)
        pltpu.make_async_remote_copy(
            src_ref=s1.at[d],
            dst_ref=r1.at[me],
            send_sem=send_sem.at[0],
            recv_sem=recv_sem.at[0],
            device_id=(lax.rem(d, G), lax.div(d, G)),
            device_id_type=MESH,
        ).start()
        return carry

    lax.fori_loop(1, N, send_state, 0)
    r1[me] = s1[me]

    for load in loads[6:9]:
        load.wait()
    for c in range(chunks):
        cut = slice(c * chunk_width, (c + 1) * chunk_width)
        res_cr[c * own : (c + 1) * own, :] = res_ref[0, :, cut].astype(f32)
        gain_cr[c * own : (c + 1) * own, :] = jnp.broadcast_to(
            gain_ref[0:1, cut], (own, chunk_width)
        )
    loads[9].wait()

    def wait_all(ref, sem):
        pltpu.make_async_copy(ref, ref, sem).wait()

    wait_all(r1.at[pl.ds(0, N - 1)], recv_sem.at[0])

    states = r1[...].astype(f32)
    weighted = states[:, :slot_rows].reshape(H, G, slot_rows, HEAD_SIZE)
    pieces = states[:, slot_rows:].reshape(N * slot_rows, HEAD_SIZE).astype(bf16)
    stats = dot(pieces, spread)
    peaks = stats[:, :HEAD_SIZE].reshape(H, G, slot_rows, HEAD_SIZE)
    masses = stats[:, HEAD_SIZE:].reshape(H, G, slot_rows, HEAD_SIZE)
    best = jnp.max(peaks, 1)
    factors = jnp.exp(peaks - best[:, None])
    attention = jnp.sum(weighted * factors, 1) / jnp.sum(masses * factors, 1)
    attention = attention.reshape(H * slot_rows, HEAD_SIZE).astype(bf16)
    by_head = dot(to_heads, attention)
    attention = jnp.concatenate(
        [by_head[i * all_rows : (i + 1) * all_rows] for i in range(heads_dev)], 1
    ).astype(bf16)

    def deal(parts):
        return dot(to_owner, jnp.concatenate(parts, 0).astype(bf16)).astype(bf16)

    shares = deal(
        [
            dot(attention, ow_ref[:, c * chunk_width : (c + 1) * chunk_width])
            for c in range(chunks)
        ]
    )
    s2[...] = shares.reshape(H, 16, chunk_width)

    def to_peers(source, target, number):
        def send(i, carry):
            d = lax.rem(h + i, H)
            pltpu.make_async_remote_copy(
                src_ref=source(d),
                dst_ref=target,
                send_sem=send_sem.at[number],
                recv_sem=recv_sem.at[number],
                device_id=(g, d),
                device_id_type=MESH,
            ).start()
            return carry

        lax.fori_loop(1, H, send, 0)

    to_peers(lambda d: s2.at[d], r2.at[h], 1)
    r2[h] = s2[h]
    gain = gain_cr[...]
    hidden = res_cr[...]
    wait_all(r2.at[pl.ds(0, H - 1)], recv_sem.at[1])

    hidden = hidden + jnp.sum(r2[...].astype(f32), 0)
    row_sums = jnp.sum(hidden * hidden, 1, keepdims=True)
    row_of = lax.rem(lax.broadcasted_iota(i32, (16, 1), 0), own)
    total = jnp.zeros((16, 1), f32)
    for r in range(own):
        one = jnp.sum(jnp.where(row_of == r, row_sums, 0.0), 0, keepdims=True)
        total = jnp.where(row_of == r, one, total)
    normed = (hidden * lax.rsqrt(total / width + norm_epsilon) * gain).astype(bf16)
    s3[...] = normed
    to_peers(lambda d: s3, r3.at[h], 2)
    r3[h] = normed
    for load in loads[10:]:
        load.wait()
    wait_all(r3.at[pl.ds(0, H - 1)], recv_sem.at[2])

    arrived = dot(to_chunks, r3[...].reshape(H * 16, chunk_width))
    arrived = jnp.concatenate(
        [arrived[c * all_rows : (c + 1) * all_rows] for c in range(chunks)], 1
    ).astype(bf16)
    for e in range(local_experts):
        gate = dot(arrived, gw_ref[e])
        up = dot(arrived, uw_ref[e])
        act = (gate / (1.0 + jnp.exp(-gate)) * up).astype(bf16)
        made = deal(
            [
                dot(act, dw_ref[e, :, c * chunk_width : (c + 1) * chunk_width])
                for c in range(chunks)
            ]
        )
        s4[e] = made.reshape(H, 16, chunk_width)
        to_peers(lambda d: s4.at[e, d], r4.at[e, h], 3 + e)
        r4[e, h] = s4[e, h]

    logits = dot(arrived, rw_ref[...])
    row_at = lax.broadcasted_iota(i32, logits.shape, 0)
    wide_row = lax.rem(lax.broadcasted_iota(i32, (16, experts), 0), own)
    wide_expert = lax.broadcasted_iota(i32, (16, experts), 1)
    ids = ids_ref[0]
    own_logits = jnp.zeros((16, experts), f32)
    chosen = jnp.zeros((16, experts), f32)
    for r in range(own):
        line = jnp.sum(jnp.where(row_at == h * own + r, logits, 0.0), 0, keepdims=True)
        own_logits = jnp.where(wide_row == r, line, own_logits)
        for c in range(TOPK):
            hit = (wide_expert == ids[r : r + 1, c : c + 1]) & (wide_row == r)
            chosen = jnp.where(hit, 1.0, chosen)
    expo = jnp.where(chosen > 0.5, jnp.exp(own_logits), 0.0)
    route = expo / jnp.sum(expo, 1, keepdims=True)

    result = hidden
    for e in range(local_experts):
        wait_all(r4.at[e, pl.ds(0, H - 1)], recv_sem.at[3 + e])
        for p in range(H):
            name = p * local_experts + e
            result = result + route[:, name : name + 1] * r4[e, p].astype(f32)
    for c in range(chunks):
        out_ref[0, :, c * chunk_width : (c + 1) * chunk_width] = result[c * own : (c + 1) * own]

    wait_all(s1.at[pl.ds(0, N - 1)], send_sem.at[0])
    wait_all(s2.at[pl.ds(0, H - 1)], send_sem.at[1])
    wait_all(r3.at[pl.ds(0, H - 1)], send_sem.at[2])
    for e in range(local_experts):
        wait_all(s4.at[e, pl.ds(0, H - 1)], send_sem.at[3 + e])


def shards(*args):
    G = lax.axis_size("grp")
    H = lax.axis_size("head")
    args = list(args)
    residual, gain = args[6], args[8]
    args[8] = gain.reshape(1, -1)
    own, width = residual.shape[1], residual.shape[2]
    chunks = 16 // own
    chunk_width = width // chunks
    slot_rows = max(8, QUERY_HEADS // H * own)
    local_experts = args[10].shape[0]
    buffers = []
    for i, a in enumerate(args):
        if i == 5:
            buffers.append(pltpu.SMEM(a.shape, a.dtype))
        else:
            buffers.append(pltpu.VMEM(a.shape, a.dtype))
    N = G * H
    state = pltpu.VMEM((N, 2 * slot_rows, HEAD_SIZE), bf16)
    share = pltpu.VMEM((H, 16, chunk_width), bf16)
    made = pltpu.VMEM((local_experts, H, 16, chunk_width), bf16)
    return pl.pallas_call(
        functools.partial(kernel, G, H),
        out_shape=jax.ShapeDtypeStruct((1, own, width), f32),
        in_specs=[pl.BlockSpec(memory_space=pl.ANY)] * len(args),
        out_specs=pl.BlockSpec(memory_space=pltpu.VMEM),
        scratch_shapes=buffers
        + [
            state,
            state,
            share,
            share,
            pltpu.VMEM((16, chunk_width), bf16),
            share,
            made,
            made,
            pltpu.VMEM((16, chunk_width), f32),
            pltpu.VMEM((16, chunk_width), f32),
            pltpu.SemaphoreType.DMA((len(args),)),
            pltpu.SemaphoreType.DMA((3 + local_experts,)),
            pltpu.SemaphoreType.DMA((3 + local_experts,)),
        ],
        compiler_params=pltpu.CompilerParams(
            collective_id=0, has_side_effects=True, vmem_limit_bytes=56 * 1024 * 1024
        ),
        name="decode_layer",
    )(*args)


def solution(mesh):
    return jax.shard_map(
        shards,
        mesh=mesh,
        in_specs=(
            P("head", None, None),
            P("head", "grp", None),
            P("head", "grp", None),
            P("head", "grp", None, None),
            P("head", "grp", None, None),
            P("head", "grp"),
            P("head", "grp", None),
            P("head", None),
            P(),
            P(),
            P("head", None, None),
            P("head", None, None),
            P("head", None, None),
            P("head", "grp", None),
        ),
        out_specs=P("head", "grp", None),
        check_vma=False,
    )
```

```python
import functools
import math

import jax
import jax.numpy as jnp
from jax import lax
from jax.experimental import pallas as pl
from jax.experimental.pallas import tpu as pltpu
from jax.sharding import PartitionSpec as P

QUERY_HEADS = 32
KEY_VALUE_HEADS = 4
HEAD_SIZE = 128
TOPK = 8

masked_score = -1e30
norm_epsilon = 1e-06
f32, bf16, i32 = jnp.float32, jnp.bfloat16, jnp.int32
MESH = pl.DeviceIdType.MESH


def dot(a, b):
    return jnp.dot(a, b, preferred_element_type=f32)


def dot_nt(a, b):
    return lax.dot_general(a, b, (((1,), (1,)), ((), ())), preferred_element_type=f32)


def one_hot(shape, source):
    a = lax.broadcasted_iota(i32, shape, 0)
    b = lax.broadcasted_iota(i32, shape, 1)
    col = lax.broadcasted_iota(i32, shape, 2)
    hit = jnp.where(source(a, b) == col, 1.0, 0.0).astype(f32)
    return hit.reshape(shape[0] * shape[1], shape[2]).astype(bf16)


def kernel(
    G,
    H,
    q_hbm,
    k_hbm,
    v_hbm,
    sk_hbm,
    sv_hbm,
    len_hbm,
    res_hbm,
    ow_hbm,
    gain_hbm,
    rw_hbm,
    gw_hbm,
    uw_hbm,
    dw_hbm,
    ids_hbm,
    out_ref,
    q_ref,
    k_ref,
    v_ref,
    sk_ref,
    sv_ref,
    len_ref,
    res_ref,
    ow_ref,
    gain_ref,
    rw_ref,
    gw_ref,
    uw_ref,
    dw_ref,
    ids_ref,
    s1,
    r1,
    s2,
    r2,
    s3,
    r3,
    s4,
    r4,
    s5,
    r5,
    gain_cr,
    res_cr,
    load_sem,
    send_sem,
    recv_sem,
):
    g = lax.axis_index("grp")
    h = lax.axis_index("head")

    rows = q_ref.shape[1]
    own = res_ref.shape[1]
    width = res_ref.shape[2]
    suffix = sk_ref.shape[2]
    group = QUERY_HEADS // KEY_VALUE_HEADS
    heads_dev = QUERY_HEADS // H
    per_group = group // heads_dev
    slot_rows = s5.shape[1] // 2
    chunks, chunk_width = 16 // own, s2.shape[2]
    all_rows = H * own
    local_experts = gw_ref.shape[0]


    pairs = [
        (q_hbm, q_ref),
        (k_hbm, k_ref),
        (len_hbm, len_ref),
        (sk_hbm, sk_ref),
        (v_hbm, v_ref),
        (sv_hbm, sv_ref),
        (res_hbm, res_ref),
        (gain_hbm, gain_ref),
        (ids_hbm, ids_ref),
        (ow_hbm, ow_ref),
        (rw_hbm, rw_ref),
        (gw_hbm, gw_ref),
        (uw_hbm, uw_ref),
        (dw_hbm, dw_ref),
    ]
    loads = [pltpu.make_async_copy(a, b, load_sem.at[i]) for i, (a, b) in enumerate(pairs)]
    for load in loads:
        load.start()

    def other_group(i):
        return (lax.rem(g + i, G), h)

    def other_head(i):
        return (g, lax.rem(h + i, H))

    barrier = pltpu.get_barrier_semaphore()
    for i in range(1, G):
        pl.semaphore_signal(barrier, inc=1, device_id=other_group(i), device_id_type=MESH)
    for i in range(1, H):
        pl.semaphore_signal(barrier, inc=1, device_id=other_head(i), device_id_type=MESH)

    def query_source(a, b):
        block, head_block = lax.div(a, per_group), lax.rem(a, per_group)
        head, row = lax.div(b, own), lax.rem(b, own)
        found = (head_block * heads_dev + head) * rows + block * own + row
        return jnp.where(b < heads_dev * own, found, -1)

    def head_source(a, b):
        offset = jnp.where(a < heads_dev, a * own, slot_rows)
        return lax.div(b, own) * 2 * slot_rows + offset + lax.rem(b, own)

    to_slots = one_hot((G * per_group, slot_rows, group * rows), query_source)
    to_heads = one_hot((heads_dev + 1, all_rows, H * 2 * slot_rows), head_source)
    to_owner = one_hot(
        (H, 16, chunks * all_rows),
        lambda a, b: lax.div(b, own) * all_rows + a * own + lax.rem(b, own),
    )
    to_chunks = one_hot(
        (chunks, all_rows, H * 16),
        lambda a, b: lax.div(b, own) * 16 + a * own + lax.rem(b, own),
    )

    for load in loads[:6]:
        load.wait()
    scale = 1.0 / math.sqrt(HEAD_SIZE)
    part = per_group * slot_rows
    count = G * part
    mask_shape = (G * per_group, slot_rows, own * suffix)
    block = lax.div(lax.broadcasted_iota(i32, mask_shape, 0), per_group)
    row = lax.rem(lax.broadcasted_iota(i32, mask_shape, 1), own)
    column = lax.broadcasted_iota(i32, mask_shape, 2)
    bound = jnp.zeros(mask_shape, i32)
    for r in range(own):
        bound = jnp.where(row == r, r * suffix + len_ref[0, r], bound)
    bound = jnp.where(block == g, bound, 0).reshape(count, own * suffix)
    first = (row * suffix).reshape(count, own * suffix)
    column = column.reshape(count, own * suffix)
    in_suffix = (column >= first) & (column < bound)
    lane = lax.broadcasted_iota(i32, (count, HEAD_SIZE), 1)
    pieces = jnp.zeros((count, HEAD_SIZE), f32)
    q32 = q_ref[0].astype(f32)
    for k in range(KEY_VALUE_HEADS):
        cut = slice(k * HEAD_SIZE, (k + 1) * HEAD_SIZE)
        stacked = jnp.concatenate(
            [
                q32[:, j * HEAD_SIZE : (j + 1) * HEAD_SIZE]
                for j in range(k * group, (k + 1) * group)
            ],
            0,
        ).astype(bf16)
        query = dot(to_slots, stacked).astype(bf16)
        scores = dot_nt(query, k_ref[0, :, cut]) * scale
        suf = dot_nt(query, sk_ref[0, :, :, cut].reshape(own * suffix, HEAD_SIZE)) * scale
        suf = jnp.where(in_suffix, suf, masked_score)
        peak = jnp.maximum(
            jnp.max(scores, -1, keepdims=True), jnp.max(suf, -1, keepdims=True)
        )
        terms = jnp.exp(scores - peak)
        suf_terms = jnp.where(in_suffix, jnp.exp(suf - peak), 0.0)
        mass = jnp.sum(terms, -1, keepdims=True) + jnp.sum(suf_terms, -1, keepdims=True)
        weighted = dot(terms.astype(bf16), v_ref[0, :, cut]) + dot(
            suf_terms.astype(bf16), sv_ref[0, :, :, cut].reshape(own * suffix, HEAD_SIZE)
        )
        s1[:, k * part : (k + 1) * part, :] = weighted.reshape(G, part, HEAD_SIZE).astype(bf16)
        at = lane - 8 * k
        value = jnp.where(at < 3, peak, mass)
        top = value.astype(bf16).astype(f32)
        rest = value - top
        middle = rest.astype(bf16).astype(f32)
        low = rest - middle
        piece = jnp.where(
            (at == 0) | (at == 3), top, jnp.where((at == 1) | (at == 4), middle, low)
        )
        pieces = jnp.where((at >= 0) & (at < 6), piece, pieces)
    s1[:, KEY_VALUE_HEADS * part :, :] = pieces.reshape(G, part, HEAD_SIZE).astype(bf16)

    pl.semaphore_wait(barrier, G + H - 2)

    for i in range(1, G):
        to = other_group(i)
        pltpu.make_async_remote_copy(
            src_ref=s1.at[to[0]],
            dst_ref=r1.at[g],
            send_sem=send_sem.at[0],
            recv_sem=recv_sem.at[0],
            device_id=to,
            device_id_type=MESH,
        ).start()
    r1[g] = s1[g]

    for load in loads[6:9]:
        load.wait()
    for c in range(chunks):
        cut = slice(c * chunk_width, (c + 1) * chunk_width)
        res_cr[c * own : (c + 1) * own, :] = res_ref[0, :, cut].astype(f32)
        gain_cr[c * own : (c + 1) * own, :] = jnp.broadcast_to(
            gain_ref[0:1, cut], (own, chunk_width)
        )
    ids = ids_ref[0].astype(f32)
    id_row = lax.rem(lax.broadcasted_iota(i32, (slot_rows, HEAD_SIZE), 0), own)
    id_lane = lax.broadcasted_iota(i32, (slot_rows, HEAD_SIZE), 1)
    id_tile = jnp.zeros((slot_rows, HEAD_SIZE), f32)
    for r in range(own):
        for c in range(TOPK):
            id_tile = jnp.where(
                (id_row == r) & (id_lane == c), ids[r : r + 1, c : c + 1], id_tile
            )
    id_tile = jnp.broadcast_to(id_tile[None], (per_group, slot_rows, HEAD_SIZE))
    stat_row = lax.broadcasted_iota(i32, (HEAD_SIZE, 2 * HEAD_SIZE), 0)
    stat_col = lax.broadcasted_iota(i32, (HEAD_SIZE, 2 * HEAD_SIZE), 1)
    stat_low = jnp.where(stat_col < HEAD_SIZE, 0, 3)

    def wait_all(ref, sem):
        pltpu.make_async_copy(ref, ref, sem).wait()

    def to_peers(source, target, number):
        for i in range(1, H):
            to = other_head(i)
            pltpu.make_async_remote_copy(
                src_ref=source(to[1]),
                dst_ref=target,
                send_sem=send_sem.at[number],
                recv_sem=recv_sem.at[number],
                device_id=to,
                device_id_type=MESH,
            ).start()

    wait_all(r1.at[pl.ds(0, G - 1)], recv_sem.at[0])

    got = r1[:, KEY_VALUE_HEADS * part :, :].reshape(count, HEAD_SIZE)
    for k in range(KEY_VALUE_HEADS):
        low = stat_low + 8 * k
        spread = jnp.where((stat_row >= low) & (stat_row < low + 3), 1.0, 0.0).astype(f32)
        stats = dot(got, spread.astype(bf16))
        peaks = stats[:, :HEAD_SIZE].reshape(G, part, HEAD_SIZE)
        masses = stats[:, HEAD_SIZE:].reshape(G, part, HEAD_SIZE)
        weighted = r1[:, k * part : (k + 1) * part, :].astype(f32)
        factors = jnp.exp(peaks - jnp.max(peaks, 0)[None])
        mine = jnp.sum(weighted * factors, 0) / jnp.sum(masses * factors, 0)
        message = jnp.concatenate([mine.reshape(per_group, slot_rows, HEAD_SIZE), id_tile], 1)
        s5[k * per_group : (k + 1) * per_group] = message.astype(bf16)
    to_peers(lambda d: s5.at[d], r5.at[h], 4)
    r5[h] = s5[h]
    loads[9].wait()
    wait_all(r5.at[pl.ds(0, H - 1)], recv_sem.at[4])
    by_head = dot(to_heads, r5[...].reshape(H * 2 * slot_rows, HEAD_SIZE))
    attention = jnp.concatenate(
        [by_head[i * all_rows : (i + 1) * all_rows] for i in range(heads_dev)], 1
    ).astype(bf16)
    all_ids = by_head[heads_dev * all_rows :]

    def deal(parts):
        return dot(to_owner, jnp.concatenate(parts, 0).astype(bf16)).astype(bf16)

    shares = deal(
        [
            dot(attention, ow_ref[:, c * chunk_width : (c + 1) * chunk_width])
            for c in range(chunks)
        ]
    )
    s2[...] = shares.reshape(H, 16, chunk_width)

    to_peers(lambda d: s2.at[d], r2.at[h], 1)
    r2[h] = s2[h]
    gain = gain_cr[...]
    hidden = res_cr[...]
    wait_all(r2.at[pl.ds(0, H - 1)], recv_sem.at[1])

    hidden = hidden + jnp.sum(r2[...].astype(f32), 0)
    row_sums = jnp.sum(hidden * hidden, 1, keepdims=True)
    row_of = lax.rem(lax.broadcasted_iota(i32, (16, 1), 0), own)
    total = jnp.zeros((16, 1), f32)
    for r in range(own):
        one = jnp.sum(jnp.where(row_of == r, row_sums, 0.0), 0, keepdims=True)
        total = jnp.where(row_of == r, one, total)
    normed = (hidden * lax.rsqrt(total / width + norm_epsilon) * gain).astype(bf16)
    s3[...] = normed
    to_peers(lambda d: s3, r3.at[h], 2)
    r3[h] = normed
    for load in loads[10:]:
        load.wait()
    wait_all(r3.at[pl.ds(0, H - 1)], recv_sem.at[2])

    arrived = dot(to_chunks, r3[...].reshape(H * 16, chunk_width))
    arrived = jnp.concatenate(
        [arrived[c * all_rows : (c + 1) * all_rows] for c in range(chunks)], 1
    ).astype(bf16)
    logits = dot_nt(arrived, rw_ref[...])
    expert_at = lax.broadcasted_iota(i32, logits.shape, 1)
    expert_at_float = expert_at.astype(f32)
    chosen = jnp.zeros(logits.shape, f32)
    for c in range(TOPK):
        chosen = jnp.where(expert_at_float == all_ids[:, c : c + 1], 1.0, chosen)
    expo = jnp.where(chosen > 0.5, jnp.exp(logits), 0.0)
    route = expo / jnp.sum(expo, 1, keepdims=True)

    mixed = [jnp.zeros((all_rows, chunk_width), f32)] * chunks
    for e in range(local_experts):
        gate = dot(arrived, gw_ref[e])
        up = dot(arrived, uw_ref[e])
        act = (gate / (1.0 + jnp.exp(-gate)) * up).astype(bf16)
        name = h * local_experts + e
        share = jnp.sum(jnp.where(expert_at == name, route, 0.0), 1, keepdims=True)
        for c in range(chunks):
            made = dot(act, dw_ref[e, :, c * chunk_width : (c + 1) * chunk_width])
            mixed[c] = mixed[c] + share * made.astype(bf16).astype(f32)
    s4[...] = deal(mixed).reshape(H, 16, chunk_width)
    to_peers(lambda d: s4.at[d], r4.at[h], 3)
    r4[h] = s4[h]
    wait_all(r4.at[pl.ds(0, H - 1)], recv_sem.at[3])
    result = hidden + jnp.sum(r4[...].astype(f32), 0)
    for c in range(chunks):
        out_ref[0, :, c * chunk_width : (c + 1) * chunk_width] = result[c * own : (c + 1) * own]

    wait_all(s1.at[pl.ds(0, G - 1)], send_sem.at[0])
    wait_all(s5.at[pl.ds(0, H - 1)], send_sem.at[4])
    wait_all(s2.at[pl.ds(0, H - 1)], send_sem.at[1])
    wait_all(r3.at[pl.ds(0, H - 1)], send_sem.at[2])
    wait_all(s4.at[pl.ds(0, H - 1)], send_sem.at[3])


def shards(*args):
    G = lax.axis_size("grp")
    H = lax.axis_size("head")
    args = list(args)
    residual, gain = args[6], args[8]
    args[8] = gain.reshape(1, -1)
    args[9] = args[9].T
    own, width = residual.shape[1], residual.shape[2]
    chunks = 16 // own
    chunk_width = width // chunks
    slot_rows = max(8, QUERY_HEADS // H * own)
    buffers = []
    for i, a in enumerate(args):
        if i == 5:
            buffers.append(pltpu.SMEM(a.shape, a.dtype))
        else:
            buffers.append(pltpu.VMEM(a.shape, a.dtype))
    per_group = QUERY_HEADS // KEY_VALUE_HEADS * H // QUERY_HEADS
    state_rows = (KEY_VALUE_HEADS + 1) * per_group * slot_rows
    state = pltpu.VMEM((G, state_rows, HEAD_SIZE), bf16)
    share = pltpu.VMEM((H, 16, chunk_width), bf16)
    slot = pltpu.VMEM((H, 2 * slot_rows, HEAD_SIZE), bf16)
    return pl.pallas_call(
        functools.partial(kernel, G, H),
        out_shape=jax.ShapeDtypeStruct((1, own, width), f32),
        in_specs=[pl.BlockSpec(memory_space=pl.ANY)] * len(args),
        out_specs=pl.BlockSpec(memory_space=pltpu.VMEM),
        scratch_shapes=buffers
        + [
            state,
            state,
            share,
            share,
            pltpu.VMEM((16, chunk_width), bf16),
            share,
            share,
            share,
            slot,
            slot,
            pltpu.VMEM((16, chunk_width), f32),
            pltpu.VMEM((16, chunk_width), f32),
            pltpu.SemaphoreType.DMA((len(args),)),
            pltpu.SemaphoreType.DMA((5,)),
            pltpu.SemaphoreType.DMA((5,)),
        ],
        compiler_params=pltpu.CompilerParams(
            collective_id=0, has_side_effects=True, vmem_limit_bytes=56 * 1024 * 1024
        ),
        name="decode_layer",
    )(*args)


def solution(mesh):
    return jax.shard_map(
        shards,
        mesh=mesh,
        in_specs=(
            P("head", None, None),
            P("head", "grp", None),
            P("head", "grp", None),
            P("head", "grp", None, None),
            P("head", "grp", None, None),
            P("head", "grp"),
            P("head", "grp", None),
            P("head", None),
            P(),
            P(),
            P("head", None, None),
            P("head", None, None),
            P("head", None, None),
            P("head", "grp", None),
        ),
        out_specs=P("head", "grp", None),
        check_vma=False,
    )
```

```python
import functools
import math

import jax
import jax.numpy as jnp
from jax import lax
from jax.experimental import pallas as pl
from jax.experimental.pallas import tpu as pltpu
from jax.sharding import PartitionSpec as P

QUERY_HEADS = 32
KEY_VALUE_HEADS = 4
HEAD_SIZE = 128
TOPK = 8

masked_score = -1e30
norm_epsilon = 1e-06
f32, bf16, i32 = jnp.float32, jnp.bfloat16, jnp.int32
MESH = pl.DeviceIdType.MESH


def dot(a, b):
    return jnp.dot(a, b, preferred_element_type=f32)


def dot_nt(a, b):
    return lax.dot_general(a, b, (((1,), (1,)), ((), ())), preferred_element_type=f32)


def div(a, n):
    return a >> (n.bit_length() - 1) if n & (n - 1) == 0 else lax.div(a, n)


def rem(a, n):
    return a & (n - 1) if n & (n - 1) == 0 else lax.rem(a, n)


def one_hot(shape, source):
    a = lax.broadcasted_iota(i32, shape, 0)
    b = lax.broadcasted_iota(i32, shape, 1)
    col = lax.broadcasted_iota(i32, shape, 2)
    hit = jnp.where(source(a, b) == col, 1.0, 0.0).astype(f32)
    return hit.reshape(shape[0] * shape[1], shape[2]).astype(bf16)


def kernel(
    G,
    H,
    q_hbm,
    k_hbm,
    v_hbm,
    sk_hbm,
    sv_hbm,
    len_hbm,
    res_hbm,
    ow_hbm,
    gain_hbm,
    rw_hbm,
    gw_hbm,
    uw_hbm,
    dw_hbm,
    ids_hbm,
    hidden_ref,
    routed_ref,
    q_ref,
    k_ref,
    v_ref,
    sk_ref,
    sv_ref,
    len_ref,
    res_ref,
    ow_ref,
    gain_ref,
    rw_ref,
    gu_ref,
    dw_ref,
    ids_ref,
    s1,
    r1,
    s2,
    r2,
    s3,
    r3,
    s4,
    r4,
    s5,
    r5,
    gain_cr,
    res_cr,
    load_sem,
    send_sem,
    recv_sem,
):
    g = lax.axis_index("grp")
    h = lax.axis_index("head")

    rows = q_ref.shape[1]
    own = res_ref.shape[1]
    width = res_ref.shape[2]
    suffix = sk_ref.shape[2]
    group = QUERY_HEADS // KEY_VALUE_HEADS
    heads_dev = QUERY_HEADS // H
    per_group = group // heads_dev
    slot_rows = s5.shape[1] // 2
    chunks, chunk_width = 16 // own, s2.shape[2]
    all_rows = H * own


    pairs = [
        (q_hbm, q_ref),
        (k_hbm, k_ref),
        (len_hbm, len_ref),
        (sk_hbm, sk_ref),
        (v_hbm, v_ref),
        (sv_hbm, sv_ref),
        (res_hbm, res_ref),
        (gain_hbm, gain_ref),
        (ids_hbm, ids_ref),
        (ow_hbm, ow_ref),
        (rw_hbm, rw_ref),
    ]
    local_experts, _, hidden_units = gw_hbm.shape
    for e in range(local_experts):
        for j, source in enumerate((gw_hbm, uw_hbm)):
            columns = pl.ds((2 * e + j) * hidden_units, hidden_units)
            pairs.append((source.at[e], gu_ref.at[:, columns]))
        pairs.append((dw_hbm.at[e], dw_ref.at[pl.ds(e * hidden_units, hidden_units)]))
    loads = [pltpu.make_async_copy(a, b, load_sem.at[i]) for i, (a, b) in enumerate(pairs)]
    for load in loads:
        load.start()

    def other_group(i):
        return (lax.rem(g + i, G), h)

    def other_head(i):
        return (g, lax.rem(h + i, H))

    barrier = pltpu.get_barrier_semaphore()
    for i in range(1, G):
        pl.semaphore_signal(barrier, inc=1, device_id=other_group(i), device_id_type=MESH)
    for i in range(1, H):
        pl.semaphore_signal(barrier, inc=1, device_id=other_head(i), device_id_type=MESH)

    def query_source(a, b):
        block, head_block = div(a, per_group), rem(a, per_group)
        head, row = div(b, own), rem(b, own)
        found = (head_block * heads_dev + head) * rows + block * own + row
        return jnp.where(b < heads_dev * own, found, -1)

    def head_source(a, b):
        offset = jnp.where(a < heads_dev, a * own, slot_rows)
        return div(b, own) * 2 * slot_rows + offset + rem(b, own)

    to_slots = one_hot((G * per_group, slot_rows, group * rows), query_source)
    to_heads = one_hot((heads_dev + 1, all_rows, H * 2 * slot_rows), head_source)
    to_owner = one_hot(
        (H, 16, chunks * all_rows),
        lambda a, b: div(b, own) * all_rows + a * own + rem(b, own),
    )
    to_chunks = one_hot(
        (chunks, all_rows, H * 16),
        lambda a, b: div(b, own) * 16 + a * own + rem(b, own),
    )

    for load in loads[:6]:
        load.wait()
    scale = 1.0 / math.sqrt(HEAD_SIZE)
    part = per_group * slot_rows
    count = G * part
    prefix = k_ref.shape[1]
    pad = -(own * suffix) % HEAD_SIZE
    padded = own * suffix + pad
    mask_shape = (G * per_group, slot_rows, padded)
    block = div(lax.broadcasted_iota(i32, mask_shape, 0), per_group)
    row = rem(lax.broadcasted_iota(i32, mask_shape, 1), own)
    column = lax.broadcasted_iota(i32, mask_shape, 2)
    bound = jnp.zeros(mask_shape, i32)
    for r in range(own):
        bound = jnp.where(row == r, r * suffix + len_ref[0, r], bound)
    bound = jnp.where(block == g, bound, 0).reshape(count, padded)
    first = (row * suffix).reshape(count, padded)
    column = column.reshape(count, padded)
    in_suffix = (column >= first) & (column < bound)
    lane = lax.broadcasted_iota(i32, (count, HEAD_SIZE), 1)
    pieces = jnp.zeros((count, HEAD_SIZE), f32)
    blank = jnp.zeros((pad, HEAD_SIZE), bf16)
    q32 = q_ref[0].astype(f32)
    for k in range(KEY_VALUE_HEADS):
        cut = slice(k * HEAD_SIZE, (k + 1) * HEAD_SIZE)
        stacked = jnp.concatenate(
            [
                q32[:, j * HEAD_SIZE : (j + 1) * HEAD_SIZE]
                for j in range(k * group, (k + 1) * group)
            ],
            0,
        ).astype(bf16)
        query = dot(to_slots, stacked).astype(bf16)
        keys = sk_ref[0, :, :, cut].reshape(own * suffix, HEAD_SIZE)
        keys = jnp.concatenate([k_ref[0, :, cut], keys, blank], 0)
        values = sv_ref[0, :, :, cut].reshape(own * suffix, HEAD_SIZE)
        values = jnp.concatenate([v_ref[0, :, cut], values, blank], 0)
        scores = dot_nt(query, keys) * scale
        suf = jnp.where(in_suffix, scores[:, prefix:], masked_score)
        scores = jnp.concatenate([scores[:, :prefix], suf], 1)
        peak = jnp.max(scores, -1, keepdims=True)
        terms = jnp.exp(scores - peak)
        suf = jnp.where(in_suffix, terms[:, prefix:], 0.0)
        terms = jnp.concatenate([terms[:, :prefix], suf], 1)
        mass = jnp.sum(terms, -1, keepdims=True)
        weighted = dot(terms.astype(bf16), values)
        s1[:, k * part : (k + 1) * part, :] = weighted.reshape(G, part, HEAD_SIZE).astype(bf16)
        at = lane - 8 * k
        value = jnp.where(at < 3, peak, mass)
        top = value.astype(bf16).astype(f32)
        rest = value - top
        middle = rest.astype(bf16).astype(f32)
        low = rest - middle
        piece = jnp.where(
            (at == 0) | (at == 3), top, jnp.where((at == 1) | (at == 4), middle, low)
        )
        pieces = jnp.where((at >= 0) & (at < 6), piece, pieces)
    s1[:, KEY_VALUE_HEADS * part :, :] = pieces.reshape(G, part, HEAD_SIZE).astype(bf16)

    pl.semaphore_wait(barrier, G + H - 2)

    for i in range(1, G):
        to = other_group(i)
        pltpu.make_async_remote_copy(
            src_ref=s1.at[to[0]],
            dst_ref=r1.at[g],
            send_sem=send_sem.at[0],
            recv_sem=recv_sem.at[0],
            device_id=to,
            device_id_type=MESH,
        ).start()
    r1[g] = s1[g]

    for load in loads[6:9]:
        load.wait()
    for c in range(chunks):
        cut = slice(c * chunk_width, (c + 1) * chunk_width)
        res_cr[c * own : (c + 1) * own, :] = res_ref[0, :, cut].astype(f32)
        gain_cr[c * own : (c + 1) * own, :] = jnp.broadcast_to(
            gain_ref[0:1, cut], (own, chunk_width)
        )
    ids = ids_ref[0].astype(f32)
    id_row = lax.rem(lax.broadcasted_iota(i32, (slot_rows, HEAD_SIZE), 0), own)
    id_lane = lax.broadcasted_iota(i32, (slot_rows, HEAD_SIZE), 1)
    id_tile = jnp.zeros((slot_rows, HEAD_SIZE), f32)
    for r in range(own):
        for c in range(TOPK):
            id_tile = jnp.where(
                (id_row == r) & (id_lane == c), ids[r : r + 1, c : c + 1], id_tile
            )
    id_tile = jnp.broadcast_to(id_tile[None], (per_group, slot_rows, HEAD_SIZE))
    stat_row = lax.broadcasted_iota(i32, (HEAD_SIZE, 2 * HEAD_SIZE), 0)
    stat_col = lax.broadcasted_iota(i32, (HEAD_SIZE, 2 * HEAD_SIZE), 1)
    stat_low = jnp.where(stat_col < HEAD_SIZE, 0, 3)

    def wait_all(ref, sem):
        pltpu.make_async_copy(ref, ref, sem).wait()

    def to_peers(source, target, number):
        for i in range(1, H):
            to = other_head(i)
            pltpu.make_async_remote_copy(
                src_ref=source(to[1]),
                dst_ref=target,
                send_sem=send_sem.at[number],
                recv_sem=recv_sem.at[number],
                device_id=to,
                device_id_type=MESH,
            ).start()

    wait_all(r1.at[pl.ds(0, G - 1)], recv_sem.at[0])

    got = r1[:, KEY_VALUE_HEADS * part :, :].reshape(count, HEAD_SIZE)
    for k in range(KEY_VALUE_HEADS):
        low = stat_low + 8 * k
        spread = jnp.where((stat_row >= low) & (stat_row < low + 3), 1.0, 0.0).astype(f32)
        stats = dot(got, spread.astype(bf16))
        peaks = stats[:, :HEAD_SIZE].reshape(G, part, HEAD_SIZE)
        masses = stats[:, HEAD_SIZE:].reshape(G, part, HEAD_SIZE)
        weighted = r1[:, k * part : (k + 1) * part, :].astype(f32)
        factors = jnp.exp(peaks - jnp.max(peaks, 0)[None])
        mine = jnp.sum(weighted * factors, 0) / jnp.sum(masses * factors, 0)
        message = jnp.concatenate([mine.reshape(per_group, slot_rows, HEAD_SIZE), id_tile], 1)
        s5[k * per_group : (k + 1) * per_group] = message.astype(bf16)
    to_peers(lambda d: s5.at[d], r5.at[h], 4)
    r5[h] = s5[h]
    loads[9].wait()
    wait_all(r5.at[pl.ds(0, H - 1)], recv_sem.at[4])
    by_head = dot(to_heads, r5[...].reshape(H * 2 * slot_rows, HEAD_SIZE))
    attention = jnp.concatenate(
        [by_head[i * all_rows : (i + 1) * all_rows] for i in range(heads_dev)], 1
    ).astype(bf16)
    all_ids = by_head[heads_dev * all_rows :]

    def deal(parts):
        return dot(to_owner, jnp.concatenate(parts, 0).astype(bf16)).astype(bf16)

    shares = deal(
        [
            dot(attention, ow_ref[:, c * chunk_width : (c + 1) * chunk_width])
            for c in range(chunks)
        ]
    )
    s2[...] = shares.reshape(H, 16, chunk_width)

    to_peers(lambda d: s2.at[d], r2.at[h], 1)
    r2[h] = s2[h]
    gain = gain_cr[...]
    hidden = res_cr[...]
    wait_all(r2.at[pl.ds(0, H - 1)], recv_sem.at[1])

    hidden = hidden + jnp.sum(r2[...].astype(f32), 0)
    row_sums = jnp.sum(hidden * hidden, 1, keepdims=True)
    row_of = lax.rem(lax.broadcasted_iota(i32, (16, 1), 0), own)
    total = jnp.zeros((16, 1), f32)
    for r in range(own):
        one = jnp.sum(jnp.where(row_of == r, row_sums, 0.0), 0, keepdims=True)
        total = jnp.where(row_of == r, one, total)
    normed = (hidden * lax.rsqrt(total / width + norm_epsilon) * gain).astype(bf16)
    s3[...] = normed
    to_peers(lambda d: s3, r3.at[h], 2)
    r3[h] = normed
    for c in range(chunks):
        cut = slice(c * chunk_width, (c + 1) * chunk_width)
        hidden_ref[0, :, cut] = hidden[c * own : (c + 1) * own]
    for load in loads[10:]:
        load.wait()
    wait_all(r3.at[pl.ds(0, H - 1)], recv_sem.at[2])

    arrived = dot(to_chunks, r3[...].reshape(H * 16, chunk_width))
    arrived = jnp.concatenate(
        [arrived[c * all_rows : (c + 1) * all_rows] for c in range(chunks)], 1
    ).astype(bf16)
    logits = dot_nt(arrived, rw_ref[...])
    expert_at = lax.broadcasted_iota(i32, logits.shape, 1)
    expert_at_float = expert_at.astype(f32)
    chosen = jnp.zeros(logits.shape, f32)
    for c in range(TOPK):
        chosen = jnp.where(expert_at_float == all_ids[:, c : c + 1], 1.0, chosen)
    expo = jnp.where(chosen > 0.5, jnp.exp(logits), 0.0)
    route = expo / jnp.sum(expo, 1, keepdims=True)

    inner = dot(arrived, gu_ref[...])
    acts = []
    for e in range(local_experts):
        gate = inner[:, 2 * e * hidden_units : (2 * e + 1) * hidden_units]
        up = inner[:, (2 * e + 1) * hidden_units : (2 * e + 2) * hidden_units]
        name = h * local_experts + e
        share = jnp.sum(jnp.where(expert_at == name, route, 0.0), 1, keepdims=True)
        acts.append((gate / (1.0 + jnp.exp(-gate)) * up * share).astype(bf16))
    acts = jnp.concatenate(acts, 1)
    mixed = [
        dot(acts, dw_ref[:, c * chunk_width : (c + 1) * chunk_width]) for c in range(chunks)
    ]
    s4[...] = deal(mixed).reshape(H, 16, chunk_width)
    to_peers(lambda d: s4.at[d], r4.at[h], 3)
    r4[h] = s4[h]
    wait_all(r4.at[pl.ds(0, H - 1)], recv_sem.at[3])
    result = jnp.sum(r4[...].astype(f32), 0)
    for c in range(chunks):
        routed_ref[0, :, c * chunk_width : (c + 1) * chunk_width] = result[c * own : (c + 1) * own]

    wait_all(s1.at[pl.ds(0, G - 1)], send_sem.at[0])
    wait_all(s5.at[pl.ds(0, H - 1)], send_sem.at[4])
    wait_all(s2.at[pl.ds(0, H - 1)], send_sem.at[1])
    wait_all(r3.at[pl.ds(0, H - 1)], send_sem.at[2])
    wait_all(s4.at[pl.ds(0, H - 1)], send_sem.at[3])


def shards(*args):
    G = lax.axis_size("grp")
    H = lax.axis_size("head")
    args = list(args)
    residual, gain = args[6], args[8]
    args[8] = gain.reshape(1, -1)
    args[9] = args[9].T
    own, width = residual.shape[1], residual.shape[2]
    chunks = 16 // own
    chunk_width = width // chunks
    slot_rows = max(8, QUERY_HEADS // H * own)
    buffers = []
    local_experts, depth, hidden_units = args[10].shape
    for i, a in enumerate(args):
        if i == 10:
            buffers.append(pltpu.VMEM((depth, 2 * local_experts * hidden_units), a.dtype))
        elif i == 11:
            continue
        elif i == 12:
            buffers.append(pltpu.VMEM((local_experts * hidden_units, width), a.dtype))
        elif i == 5:
            buffers.append(pltpu.SMEM(a.shape, a.dtype))
        else:
            buffers.append(pltpu.VMEM(a.shape, a.dtype))
    per_group = QUERY_HEADS // KEY_VALUE_HEADS * H // QUERY_HEADS
    state_rows = (KEY_VALUE_HEADS + 1) * per_group * slot_rows
    state = pltpu.VMEM((G, state_rows, HEAD_SIZE), bf16)
    share = pltpu.VMEM((H, 16, chunk_width), bf16)
    slot = pltpu.VMEM((H, 2 * slot_rows, HEAD_SIZE), bf16)
    part = pltpu.VMEM((1, own, width), f32)
    hidden, routed = pl.pallas_call(
        functools.partial(kernel, G, H),
        out_shape=(part, part),
        in_specs=[pl.BlockSpec(memory_space=pl.ANY)] * len(args),
        out_specs=[pl.BlockSpec(memory_space=pltpu.VMEM)] * 2,
        scratch_shapes=buffers
        + [
            state,
            state,
            share,
            share,
            pltpu.VMEM((16, chunk_width), bf16),
            share,
            share,
            share,
            slot,
            slot,
            pltpu.VMEM((16, chunk_width), f32),
            pltpu.VMEM((16, chunk_width), f32),
            pltpu.SemaphoreType.DMA((len(args) - 3 + 3 * local_experts,)),
            pltpu.SemaphoreType.DMA((5,)),
            pltpu.SemaphoreType.DMA((5,)),
        ],
        compiler_params=pltpu.CompilerParams(
            collective_id=0, has_side_effects=True, vmem_limit_bytes=56 * 1024 * 1024
        ),
        name="decode_layer",
    )(*args)
    return hidden + routed


def solution(mesh):
    return jax.shard_map(
        shards,
        mesh=mesh,
        in_specs=(
            P("head", None, None),
            P("head", "grp", None),
            P("head", "grp", None),
            P("head", "grp", None, None),
            P("head", "grp", None, None),
            P("head", "grp"),
            P("head", "grp", None),
            P("head", None),
            P(),
            P(),
            P("head", None, None),
            P("head", None, None),
            P("head", None, None),
            P("head", "grp", None),
        ),
        out_specs=P("head", "grp", None),
        check_vma=False,
    )
```

```python
import functools
import math

import jax
import jax.numpy as jnp
from jax import lax
from jax.experimental import pallas as pl
from jax.experimental.pallas import tpu as pltpu
from jax.sharding import PartitionSpec as P

QUERY_HEADS = 32
KEY_VALUE_HEADS = 4
HEAD_SIZE = 128
TOPK = 8

masked_score = -1e30
norm_epsilon = 1e-06
f32, bf16, i32 = jnp.float32, jnp.bfloat16, jnp.int32
MESH = pl.DeviceIdType.MESH


def dot(a, b):
    return jnp.dot(a, b, preferred_element_type=f32)


def dot_nt(a, b):
    return lax.dot_general(a, b, (((1,), (1,)), ((), ())), preferred_element_type=f32)


def div(a, n):
    return a >> (n.bit_length() - 1) if n & (n - 1) == 0 else lax.div(a, n)


def rem(a, n):
    return a & (n - 1) if n & (n - 1) == 0 else lax.rem(a, n)


def one_hot(shape, source):
    a = lax.broadcasted_iota(i32, shape, 0)
    b = lax.broadcasted_iota(i32, shape, 1)
    col = lax.broadcasted_iota(i32, shape, 2)
    hit = jnp.where(source(a, b) == col, 1.0, 0.0).astype(f32)
    return hit.reshape(shape[0] * shape[1], shape[2]).astype(bf16)


def kernel(
    G,
    H,
    q_hbm,
    k_hbm,
    v_hbm,
    sk_hbm,
    sv_hbm,
    len_hbm,
    res_hbm,
    ow_hbm,
    gain_hbm,
    rw_hbm,
    gw_hbm,
    uw_hbm,
    dw_hbm,
    ids_hbm,
    hidden_ref,
    routed_ref,
    q_ref,
    k_ref,
    v_ref,
    sk_ref,
    sv_ref,
    len_ref,
    res_ref,
    ow_ref,
    gain_ref,
    rw_ref,
    gu_ref,
    dw_ref,
    ids_ref,
    s1,
    r1,
    s2,
    r2,
    s3,
    r3,
    s4,
    r4,
    s5,
    r5,
    gain_cr,
    res_cr,
    load_sem,
    send_sem,
    recv_sem,
):
    g = lax.axis_index("grp")
    h = lax.axis_index("head")

    rows = q_ref.shape[1]
    own = res_ref.shape[1]
    width = res_ref.shape[2]
    suffix = sk_ref.shape[2]
    group = QUERY_HEADS // KEY_VALUE_HEADS
    heads_dev = QUERY_HEADS // H
    per_group = group // heads_dev
    slot_rows = s5.shape[1] // 2
    chunks, chunk_width = 16 // own, s2.shape[2]
    all_rows = H * own


    pairs = [
        (q_hbm, q_ref),
        (k_hbm, k_ref),
        (len_hbm, len_ref),
        (sk_hbm, sk_ref),
        (v_hbm, v_ref),
        (sv_hbm, sv_ref),
        (res_hbm, res_ref),
        (gain_hbm, gain_ref),
        (ids_hbm, ids_ref),
        (ow_hbm, ow_ref),
        (rw_hbm, rw_ref),
    ]
    local_experts, _, hidden_units = gw_hbm.shape
    for e in range(local_experts):
        for j, source in enumerate((gw_hbm, uw_hbm)):
            columns = pl.ds((2 * e + j) * hidden_units, hidden_units)
            pairs.append((source.at[e], gu_ref.at[:, columns]))
        pairs.append((dw_hbm.at[e], dw_ref.at[pl.ds(e * hidden_units, hidden_units)]))
    loads = [pltpu.make_async_copy(a, b, load_sem.at[i]) for i, (a, b) in enumerate(pairs)]
    for load in loads[:9]:
        load.start()

    def other_group(i):
        return (lax.rem(g + i, G), h)

    def other_head(i):
        return (g, lax.rem(h + i, H))

    barrier = pltpu.get_barrier_semaphore()
    for i in range(1, G):
        pl.semaphore_signal(barrier, inc=1, device_id=other_group(i), device_id_type=MESH)
    for i in range(1, H):
        pl.semaphore_signal(barrier, inc=1, device_id=other_head(i), device_id_type=MESH)

    def query_source(a, b):
        block, head_block = div(a, per_group), rem(a, per_group)
        head, row = div(b, own), rem(b, own)
        found = (head_block * heads_dev + head) * rows + block * own + row
        return jnp.where(b < heads_dev * own, found, -1)

    def head_source(a, b):
        offset = jnp.where(a < heads_dev, a * own, slot_rows)
        return div(b, own) * 2 * slot_rows + offset + rem(b, own)

    to_slots = one_hot((G * per_group, slot_rows, group * rows), query_source)
    to_heads = one_hot((heads_dev + 1, all_rows, H * 2 * slot_rows), head_source)
    to_owner = one_hot(
        (H, 16, chunks * all_rows),
        lambda a, b: div(b, own) * all_rows + a * own + rem(b, own),
    )
    to_chunks = one_hot(
        (chunks, all_rows, H * 16),
        lambda a, b: div(b, own) * 16 + a * own + rem(b, own),
    )

    for load in loads[:6]:
        load.wait()
    loads[9].start()
    scale = 1.0 / math.sqrt(HEAD_SIZE)
    part = per_group * slot_rows
    count = G * part
    prefix = k_ref.shape[1]
    pad = -(own * suffix) % HEAD_SIZE
    padded = own * suffix + pad
    mask_shape = (G * per_group, slot_rows, padded)
    block = div(lax.broadcasted_iota(i32, mask_shape, 0), per_group)
    row = rem(lax.broadcasted_iota(i32, mask_shape, 1), own)
    column = lax.broadcasted_iota(i32, mask_shape, 2)
    bound = jnp.zeros(mask_shape, i32)
    for r in range(own):
        bound = jnp.where(row == r, r * suffix + len_ref[0, r], bound)
    bound = jnp.where(block == g, bound, 0).reshape(count, padded)
    first = (row * suffix).reshape(count, padded)
    column = column.reshape(count, padded)
    in_suffix = (column >= first) & (column < bound)
    lane = lax.broadcasted_iota(i32, (count, HEAD_SIZE), 1)
    pieces = jnp.zeros((count, HEAD_SIZE), f32)
    blank = jnp.zeros((pad, HEAD_SIZE), bf16)
    q32 = q_ref[0].astype(f32)
    for k in range(KEY_VALUE_HEADS):
        cut = slice(k * HEAD_SIZE, (k + 1) * HEAD_SIZE)
        stacked = jnp.concatenate(
            [
                q32[:, j * HEAD_SIZE : (j + 1) * HEAD_SIZE]
                for j in range(k * group, (k + 1) * group)
            ],
            0,
        ).astype(bf16)
        query = dot(to_slots, stacked).astype(bf16)
        keys = sk_ref[0, :, :, cut].reshape(own * suffix, HEAD_SIZE)
        keys = jnp.concatenate([k_ref[0, :, cut], keys, blank], 0)
        values = sv_ref[0, :, :, cut].reshape(own * suffix, HEAD_SIZE)
        values = jnp.concatenate([v_ref[0, :, cut], values, blank], 0)
        scores = dot_nt(query, keys) * scale
        suf = jnp.where(in_suffix, scores[:, prefix:], masked_score)
        scores = jnp.concatenate([scores[:, :prefix], suf], 1)
        peak = jnp.max(scores, -1, keepdims=True)
        terms = jnp.exp(scores - peak)
        suf = jnp.where(in_suffix, terms[:, prefix:], 0.0)
        terms = jnp.concatenate([terms[:, :prefix], suf], 1)
        mass = jnp.sum(terms, -1, keepdims=True)
        weighted = dot(terms.astype(bf16), values)
        s1[:, k * part : (k + 1) * part, :] = weighted.reshape(G, part, HEAD_SIZE).astype(bf16)
        at = lane - 8 * k
        value = jnp.where(at < 3, peak, mass)
        top = value.astype(bf16).astype(f32)
        rest = value - top
        middle = rest.astype(bf16).astype(f32)
        low = rest - middle
        piece = jnp.where(
            (at == 0) | (at == 3), top, jnp.where((at == 1) | (at == 4), middle, low)
        )
        pieces = jnp.where((at >= 0) & (at < 6), piece, pieces)
    s1[:, KEY_VALUE_HEADS * part :, :] = pieces.reshape(G, part, HEAD_SIZE).astype(bf16)

    pl.semaphore_wait(barrier, G + H - 2)

    for i in range(1, G):
        to = other_group(i)
        pltpu.make_async_remote_copy(
            src_ref=s1.at[to[0]],
            dst_ref=r1.at[g],
            send_sem=send_sem.at[0],
            recv_sem=recv_sem.at[0],
            device_id=to,
            device_id_type=MESH,
        ).start()
    for load in loads[10:]:
        load.start()
    r1[g] = s1[g]

    for load in loads[6:9]:
        load.wait()
    for c in range(chunks):
        cut = slice(c * chunk_width, (c + 1) * chunk_width)
        res_cr[c * own : (c + 1) * own, :] = res_ref[0, :, cut].astype(f32)
        gain_cr[c * own : (c + 1) * own, :] = jnp.broadcast_to(
            gain_ref[0:1, cut], (own, chunk_width)
        )
    ids = ids_ref[0].astype(f32)
    id_row = lax.rem(lax.broadcasted_iota(i32, (slot_rows, HEAD_SIZE), 0), own)
    id_lane = lax.broadcasted_iota(i32, (slot_rows, HEAD_SIZE), 1)
    id_tile = jnp.zeros((slot_rows, HEAD_SIZE), f32)
    for r in range(own):
        for c in range(TOPK):
            id_tile = jnp.where(
                (id_row == r) & (id_lane == c), ids[r : r + 1, c : c + 1], id_tile
            )
    id_tile = jnp.broadcast_to(id_tile[None], (per_group, slot_rows, HEAD_SIZE))
    stat_row = lax.broadcasted_iota(i32, (HEAD_SIZE, 2 * HEAD_SIZE), 0)
    stat_col = lax.broadcasted_iota(i32, (HEAD_SIZE, 2 * HEAD_SIZE), 1)
    stat_low = jnp.where(stat_col < HEAD_SIZE, 0, 3)

    def wait_all(ref, sem):
        pltpu.make_async_copy(ref, ref, sem).wait()

    def to_peers(source, target, number):
        for i in sorted(range(1, H), key=lambda i: abs(i - H // 2)):
            to = other_head(i)
            pltpu.make_async_remote_copy(
                src_ref=source(to[1]),
                dst_ref=target,
                send_sem=send_sem.at[number],
                recv_sem=recv_sem.at[number],
                device_id=to,
                device_id_type=MESH,
            ).start()

    wait_all(r1.at[pl.ds(0, G - 1)], recv_sem.at[0])

    got = r1[:, KEY_VALUE_HEADS * part :, :].reshape(count, HEAD_SIZE)
    for k in range(KEY_VALUE_HEADS):
        low = stat_low + 8 * k
        spread = jnp.where((stat_row >= low) & (stat_row < low + 3), 1.0, 0.0).astype(f32)
        stats = dot(got, spread.astype(bf16))
        peaks = stats[:, :HEAD_SIZE].reshape(G, part, HEAD_SIZE)
        masses = stats[:, HEAD_SIZE:].reshape(G, part, HEAD_SIZE)
        weighted = r1[:, k * part : (k + 1) * part, :].astype(f32)
        factors = jnp.exp(peaks - jnp.max(peaks, 0)[None])
        mine = jnp.sum(weighted * factors, 0) / jnp.sum(masses * factors, 0)
        message = jnp.concatenate([mine.reshape(per_group, slot_rows, HEAD_SIZE), id_tile], 1)
        s5[k * per_group : (k + 1) * per_group] = message.astype(bf16)
    to_peers(lambda d: s5.at[d], r5.at[h], 4)
    r5[h] = s5[h]
    loads[9].wait()
    wait_all(r5.at[pl.ds(0, H - 1)], recv_sem.at[4])
    by_head = dot(to_heads, r5[...].reshape(H * 2 * slot_rows, HEAD_SIZE))
    attention = jnp.concatenate(
        [by_head[i * all_rows : (i + 1) * all_rows] for i in range(heads_dev)], 1
    ).astype(bf16)
    all_ids = by_head[heads_dev * all_rows :]

    def deal(parts):
        return dot(to_owner, jnp.concatenate(parts, 0).astype(bf16)).astype(bf16)

    shares = deal(
        [
            dot(attention, ow_ref[:, c * chunk_width : (c + 1) * chunk_width])
            for c in range(chunks)
        ]
    )
    s2[...] = shares.reshape(H, 16, chunk_width)

    to_peers(lambda d: s2.at[d], r2.at[h], 1)
    r2[h] = s2[h]
    gain = gain_cr[...]
    hidden = res_cr[...]
    wait_all(r2.at[pl.ds(0, H - 1)], recv_sem.at[1])

    hidden = hidden + jnp.sum(r2[...].astype(f32), 0)
    row_sums = jnp.sum(hidden * hidden, 1, keepdims=True)
    row_of = lax.rem(lax.broadcasted_iota(i32, (16, 1), 0), own)
    total = jnp.zeros((16, 1), f32)
    for r in range(own):
        one = jnp.sum(jnp.where(row_of == r, row_sums, 0.0), 0, keepdims=True)
        total = jnp.where(row_of == r, one, total)
    normed = (hidden * lax.rsqrt(total / width + norm_epsilon) * gain).astype(bf16)
    s3[...] = normed
    to_peers(lambda d: s3, r3.at[h], 2)
    r3[h] = normed
    for c in range(chunks):
        cut = slice(c * chunk_width, (c + 1) * chunk_width)
        hidden_ref[0, :, cut] = hidden[c * own : (c + 1) * own]
    for load in loads[10:]:
        load.wait()
    wait_all(r3.at[pl.ds(0, H - 1)], recv_sem.at[2])

    arrived = dot(to_chunks, r3[...].reshape(H * 16, chunk_width))
    arrived = jnp.concatenate(
        [arrived[c * all_rows : (c + 1) * all_rows] for c in range(chunks)], 1
    ).astype(bf16)
    logits = dot_nt(arrived, rw_ref[...])
    expert_at = lax.broadcasted_iota(i32, logits.shape, 1)
    expert_at_float = expert_at.astype(f32)
    chosen = jnp.zeros(logits.shape, f32)
    for c in range(TOPK):
        chosen = jnp.where(expert_at_float == all_ids[:, c : c + 1], 1.0, chosen)
    expo = jnp.where(chosen > 0.5, jnp.exp(logits), 0.0)
    route = expo / jnp.sum(expo, 1, keepdims=True)

    inner = dot(arrived, gu_ref[...])
    acts = []
    for e in range(local_experts):
        gate = inner[:, 2 * e * hidden_units : (2 * e + 1) * hidden_units]
        up = inner[:, (2 * e + 1) * hidden_units : (2 * e + 2) * hidden_units]
        name = h * local_experts + e
        share = jnp.sum(jnp.where(expert_at == name, route, 0.0), 1, keepdims=True)
        acts.append((gate / (1.0 + jnp.exp(-gate)) * up * share).astype(bf16))
    acts = jnp.concatenate(acts, 1)
    mixed = [
        dot(acts, dw_ref[:, c * chunk_width : (c + 1) * chunk_width]) for c in range(chunks)
    ]
    s4[...] = deal(mixed).reshape(H, 16, chunk_width)
    to_peers(lambda d: s4.at[d], r4.at[h], 3)
    r4[h] = s4[h]
    wait_all(r4.at[pl.ds(0, H - 1)], recv_sem.at[3])
    result = jnp.sum(r4[...].astype(f32), 0)
    for c in range(chunks):
        routed_ref[0, :, c * chunk_width : (c + 1) * chunk_width] = result[c * own : (c + 1) * own]

    wait_all(s1.at[pl.ds(0, G - 1)], send_sem.at[0])
    wait_all(s5.at[pl.ds(0, H - 1)], send_sem.at[4])
    wait_all(s2.at[pl.ds(0, H - 1)], send_sem.at[1])
    wait_all(r3.at[pl.ds(0, H - 1)], send_sem.at[2])
    wait_all(s4.at[pl.ds(0, H - 1)], send_sem.at[3])


def shards(*args):
    G = lax.axis_size("grp")
    H = lax.axis_size("head")
    args = list(args)
    residual, gain = args[6], args[8]
    args[8] = gain.reshape(1, -1)
    args[9] = args[9].T
    own, width = residual.shape[1], residual.shape[2]
    chunks = 16 // own
    chunk_width = width // chunks
    slot_rows = max(8, QUERY_HEADS // H * own)
    buffers = []
    local_experts, depth, hidden_units = args[10].shape
    for i, a in enumerate(args):
        if i == 10:
            buffers.append(pltpu.VMEM((depth, 2 * local_experts * hidden_units), a.dtype))
        elif i == 11:
            continue
        elif i == 12:
            buffers.append(pltpu.VMEM((local_experts * hidden_units, width), a.dtype))
        elif i == 5:
            buffers.append(pltpu.SMEM(a.shape, a.dtype))
        else:
            buffers.append(pltpu.VMEM(a.shape, a.dtype))
    per_group = QUERY_HEADS // KEY_VALUE_HEADS * H // QUERY_HEADS
    state_rows = (KEY_VALUE_HEADS + 1) * per_group * slot_rows
    state = pltpu.VMEM((G, state_rows, HEAD_SIZE), bf16)
    share = pltpu.VMEM((H, 16, chunk_width), bf16)
    slot = pltpu.VMEM((H, 2 * slot_rows, HEAD_SIZE), bf16)
    part = pltpu.VMEM((1, own, width), f32)
    hidden, routed = pl.pallas_call(
        functools.partial(kernel, G, H),
        out_shape=(part, part),
        in_specs=[pl.BlockSpec(memory_space=pl.ANY)] * len(args),
        out_specs=[pl.BlockSpec(memory_space=pltpu.VMEM)] * 2,
        scratch_shapes=buffers
        + [
            state,
            state,
            share,
            share,
            pltpu.VMEM((16, chunk_width), bf16),
            share,
            share,
            share,
            slot,
            slot,
            pltpu.VMEM((16, chunk_width), f32),
            pltpu.VMEM((16, chunk_width), f32),
            pltpu.SemaphoreType.DMA((len(args) - 3 + 3 * local_experts,)),
            pltpu.SemaphoreType.DMA((5,)),
            pltpu.SemaphoreType.DMA((5,)),
        ],
        compiler_params=pltpu.CompilerParams(
            collective_id=0, has_side_effects=True, vmem_limit_bytes=56 * 1024 * 1024
        ),
        name="decode_layer",
    )(*args)
    return hidden + routed


def solution(mesh):
    return jax.shard_map(
        shards,
        mesh=mesh,
        in_specs=(
            P("head", None, None),
            P("head", "grp", None),
            P("head", "grp", None),
            P("head", "grp", None, None),
            P("head", "grp", None, None),
            P("head", "grp"),
            P("head", "grp", None),
            P("head", None),
            P(),
            P(),
            P("head", None, None),
            P("head", None, None),
            P("head", None, None),
            P("head", "grp", None),
        ),
        out_specs=P("head", "grp", None),
        check_vma=False,
    )
```
